32 devices in a mesh: groups: 2 (over y), tensor: 16 (over z, x, core).
Axes of the slice: x: 2, y: 2, z: 4, core: 2. Of those that a mesh axis runs over, the one named last changes fastest.
Arguments:
- token_ids: int32 [64], P(('groups', 'tensor')), parts along dimension 0, may hold values from 0 to 17
- return_ids: int32 [64], P(('groups', 'tensor')), parts along dimension 0, may hold values from 0 to 63
- token_table: bfloat16 [18, 8192], replicated, may hold values from -6 to 6
- return_table: bfloat16 [64, 8192], replicated, may hold values from -6 to 6
- norm_gain: float32 [8192], replicated, may hold values from 0.1 to 1.9
- gate_weight: bfloat16 [8192, 29568], P(None, 'tensor'), may hold values from -0.0625 to 0.0625
- up_weight: bfloat16 [8192, 29568], P(None, 'tensor'), may hold values from -0.0625 to 0.0625
- down_weight: bfloat16 [29568, 8192], P('tensor'), may hold values from -0.03125 to 0.03125
Outputs:
- mixed: bfloat16 [64, 8192], P(('groups', 'tensor')), parts along dimension 0
The draws below stay inside these ranges and needn't reach their ends.
There are 2 independent parts, one for each index of `groups`. The reference program is written for one: setup_inputs(seed, part) draws one part's arguments, and reference() takes and returns one part's arrays. A program takes and returns all parts, laid end to end along the dimension named above; an argument that names none is the same for every part. Nothing has to cross between parts.
All inputs are finite; a program needn't handle non-finite values.
Results may differ from the reference program's by a relative error of at most 0.0064.
Values may be sent and summed in bfloat16 or wider, within the bound.
A program may use at most 192 MiB of HBM per device.

```python
import jax
import jax.numpy as jnp
from jax import lax

D = 8192
FF = 29568
VOCAB = 18
BUCKETS = 64
TOKENS = 32


def with_ends(array, own_key, smallest, top_value):
    index_at = [jax.random.randint(jax.random.fold_in(own_key, axis), (), 0, length) for axis, length in enumerate(array.shape)]
    main_axis = array.shape.index(max(array.shape))
    neighbour = index_at[:main_axis] + [(index_at[main_axis] + 1) % array.shape[main_axis]] + index_at[main_axis + 1:]
    return array.at[tuple(index_at)].set(smallest).at[tuple(neighbour)].set(top_value)


def steps_of(key, extent, pieces, least, high):
    factor_of = 1.0
    for position, blocks in pieces:
        draws = jax.random.uniform(jax.random.fold_in(jax.random.fold_in(key, 6), position), (blocks,), jnp.float32, least / len(pieces), high / len(pieces))
        factor_of = factor_of * jnp.repeat(jnp.exp(draws), extent[position] // blocks).reshape((-1,) + (1,) * (len(extent) - 1 - position))
    return factor_of


def noise(rng, shape, width, limit, shards=(), held_as=jnp.bfloat16):
    gain = steps_of(rng, shape, shards, -0.22, 0.18) if shards else 1.0
    entries = jax.random.normal(rng, shape, jnp.float32) * width * gain
    return jnp.minimum(jnp.maximum(entries, -limit), limit).astype(held_as)


def setup_inputs(seed: int = 0, part: int = 0) -> dict:
    keys = jax.random.split(jax.random.key(seed), 9)
    part_splits = jax.random.split(jax.random.fold_in(keys[8], part), 9)
    return {
        "token_ids": with_ends(jax.random.randint(part_splits[0], (TOKENS,), 0, VOCAB), jax.random.fold_in(part_splits[0], 1), 0, VOCAB - 1).astype(jnp.int32),
        "return_ids": with_ends(jax.random.randint(part_splits[1], (TOKENS,), 0, BUCKETS), jax.random.fold_in(part_splits[1], 1), 0, BUCKETS - 1).astype(jnp.int32),
        "token_table": noise(keys[2], (VOCAB, D), 1.0, 6.0),
        "return_table": noise(keys[3], (BUCKETS, D), 1.0, 6.0),
        "norm_gain": jnp.clip(1.0 + 0.18 * jax.random.normal(keys[4], (D,), jnp.float32), 0.1, 1.9),
        "gate_weight": noise(keys[5], (D, FF), D ** -0.5, 0.0625, ((1, 16),)),
        "up_weight": noise(keys[6], (D, FF), D ** -0.5, 0.0625, ((1, 16),)),
        "down_weight": noise(keys[7], (FF, D), FF ** -0.5, 0.03125, ((0, 16),)),
    }


def reference(token_ids, return_ids, token_table, return_table, norm_gain, gate_weight, up_weight, down_weight):
    stream = token_table[token_ids].astype(jnp.float32) + return_table[return_ids].astype(jnp.float32)
    scale = jax.lax.rsqrt(lax.optimization_barrier(jnp.mean(stream * stream, axis=1, keepdims=True)) + 1e-06)
    normed = (stream * scale * norm_gain[None, :]).astype(jnp.bfloat16)
    gate = jnp.dot(normed, gate_weight, preferred_element_type=jnp.float32)
    up_value = jnp.dot(normed, up_weight, preferred_element_type=jnp.float32)
    hidden = (jax.nn.silu(gate) * up_value).astype(jnp.bfloat16)
    return jnp.dot(hidden, down_weight, preferred_element_type=jnp.float32).astype(jnp.bfloat16)
```

```python
import functools

import jax
import jax.numpy as jnp
from jax import lax
from jax.experimental import pallas as pl
from jax.experimental.pallas import tpu as pltpu
from jax.sharding import PartitionSpec as P

MESH = pl.DeviceIdType.MESH
F32 = jnp.float32
BF16 = jnp.bfloat16
WIDE = 512
SLOT_BYTES = 50 * 1024 * 1024


def up_to(value, step):
    return -(-value // step) * step


def kernel(
    n,
    slots,
    tok_hbm,
    ret_hbm,
    tt_hbm,
    rt_hbm,
    gain_hbm,
    gate_hbm,
    up_hbm,
    down_hbm,
    out_ref,
    tok_s,
    ret_s,
    tt,
    rt,
    gain,
    idbuf,
    stream,
    normed,
    weights,
    acc_g,
    acc_u,
    hidden,
    part,
    crecv,
    turned,
    own,
    sbuf,
    rbuf,
    local_sem,
    w_sem,
    id_send,
    id_recv,
    core_send,
    core_recv,
    chip_send,
    chip_recv,
):
    me = lax.axis_index("tensor")
    core = lax.rem(me, 2)
    chip = lax.div(me, 2)
    partner = me + 1 - 2 * core
    chips = n // 2
    rows = tok_hbm.shape[0]
    tokens = rows * n
    half = tokens // 2
    d = gain.shape[1]
    pairs = d // WIDE
    chunk = 2 * WIDE
    chunks = d // chunk
    lanes = idbuf.shape[2]
    per = 16 // rows

    tok_copy = pltpu.make_async_copy(tok_hbm, tok_s, local_sem.at[0])
    ret_copy = pltpu.make_async_copy(ret_hbm, ret_s, local_sem.at[1])
    tt_copy = pltpu.make_async_copy(tt_hbm, tt, local_sem.at[2])
    rt_copy = pltpu.make_async_copy(rt_hbm, rt, local_sem.at[3])
    gain_copy = pltpu.make_async_copy(gain_hbm, gain, local_sem.at[4])
    tok_copy.start()
    ret_copy.start()

    barrier = pltpu.get_barrier_semaphore()

    def greet(k, carry):
        pl.semaphore_signal(
            barrier, inc=1, device_id={"tensor": lax.rem(me + k, n)}, device_id_type=MESH
        )
        return carry

    lax.fori_loop(1, n, greet, 0)
    tt_copy.start()
    rt_copy.start()
    gain_copy.start()

    def piece(ref, t, slot, which):
        at = pl.ds(pl.multiple_of(t * WIDE, WIDE), WIDE)
        return pltpu.make_async_copy(
            ref.at[:, at], weights.at[slot, which], w_sem.at[slot, which]
        )

    def start_gate_up(t):
        slot = lax.rem(t, slots)
        piece(gate_hbm, t, slot, 0).start()
        piece(up_hbm, t, slot, 1).start()

    def start_down(t):
        slot = lax.rem(t + pairs, slots)
        piece(down_hbm, 2 * t, slot, 0).start()
        piece(down_hbm, 2 * t + 1, slot, 1).start()

    for t in range(slots):
        if t < pairs:
            start_gate_up(jnp.int32(t))
        else:
            start_down(jnp.int32(t - pairs))

    tok_copy.wait()
    ret_copy.wait()
    lane = lax.broadcasted_iota(jnp.int32, (1, lanes), 1)
    place = core * half + chip * rows
    for kind, ids in ((0, tok_s), (1, ret_s)):
        row = jnp.zeros((1, lanes), jnp.int32)
        for i in range(rows):
            row = jnp.where(lane == place + i, ids[i], row)
        idbuf[n - 1, kind : kind + 1, :] = row

    pl.semaphore_wait(barrier, n - 1)

    def send_ids(k, carry):
        pltpu.make_async_remote_copy(
            src_ref=idbuf.at[n - 1],
            dst_ref=idbuf.at[k - 1],
            send_sem=id_send,
            recv_sem=id_recv,
            device_id={"tensor": lax.rem(me + k, n)},
            device_id_type=MESH,
        ).start()
        return carry

    lax.fori_loop(1, n, send_ids, 0)
    tt_copy.wait()
    rt_copy.wait()
    gain_copy.wait()
    others = idbuf.at[pl.ds(0, n - 1)]
    pltpu.make_async_copy(others, others, id_recv).wait()
    both = jnp.sum(idbuf[...], axis=0)

    def one_hot(row, size):
        key = lax.broadcasted_iota(jnp.int32, (128, lanes), 0)
        hot = jnp.where(key == jnp.broadcast_to(row, (128, lanes)), 1.0, 0.0).astype(F32)
        return jnp.transpose(hot)[:tokens, :size].astype(BF16)

    tok_hot = one_hot(both[0:1], tt.shape[0])
    ret_hot = one_hot(both[1:2], rt.shape[0])
    total = jnp.zeros((tokens, 1), F32)
    for c in range(chunks):
        at = slice(c * chunk, (c + 1) * chunk)
        value = jnp.dot(tok_hot, tt[:, at], preferred_element_type=F32) + jnp.dot(
            ret_hot, rt[:, at], preferred_element_type=F32
        )
        stream[:, at] = value
        total += jnp.sum(value * value, axis=1, keepdims=True)
    scale = lax.rsqrt(total / d + 1e-06)
    for c in range(chunks):
        at = slice(c * chunk, (c + 1) * chunk)
        normed[:, at] = (stream[:, at] * scale * gain[:, at]).astype(BF16)

    acc_g[...] = jnp.zeros_like(acc_g)
    acc_u[...] = jnp.zeros_like(acc_u)

    def gate_up(t, carry):
        slot = lax.rem(t, slots)
        x = normed[:, pl.ds(pl.multiple_of(t * WIDE, WIDE), WIDE)]
        for which, ref, acc in ((0, gate_hbm, acc_g), (1, up_hbm, acc_u)):
            piece(ref, t, slot, which).wait()
            acc[...] += lax.dot_general(
                x, weights[slot, which], (((1,), (1,)), ((), ())), preferred_element_type=F32
            )
        ahead = t + slots

        @pl.when(ahead < pairs)
        def _():
            start_gate_up(ahead)

        @pl.when(jnp.logical_and(ahead >= pairs, ahead < pairs + chunks))
        def _():
            start_down(ahead - pairs)

        return carry

    lax.fori_loop(0, pairs, gate_up, 0)
    gate = acc_g[...]
    hidden[...] = (gate / (1.0 + jnp.exp(-gate)) * acc_u[...]).astype(BF16)

    def core_copy(c):
        return pltpu.make_async_remote_copy(
            src_ref=part.at[c, 1 - core],
            dst_ref=crecv.at[c],
            send_sem=core_send.at[c],
            recv_sem=core_recv.at[c],
            device_id={"tensor": partner},
            device_id_type=MESH,
        )

    def project(c):
        slot = lax.rem(c + pairs, slots)
        for which in range(2):
            piece(down_hbm, 2 * c + which, slot, which).wait()
            value = jnp.dot(hidden[...], weights[slot, which], preferred_element_type=F32)
            at = slice(which * WIDE, (which + 1) * WIDE)
            part[c, 0, :, at] = value[:half]
            part[c, 1, :, at] = value[half:]
        core_copy(c).start()

    def spread(c):
        core_copy(c).wait_recv()
        mine = part.at[c, core]
        mine[...] += crecv[c]

        def turn(j):
            for q in range(per):
                turned[j, q * rows : (q + 1) * rows, :] = mine[
                    j * rows : (j + 1) * rows, q * 128 : (q + 1) * 128
                ]

        for j in range(chips):
            turn(j)
        own[c] = turned[chip]
        sbuf[c] = turned[...].astype(BF16)

        def send(k, carry):
            to = lax.rem(chip + k, chips)
            pltpu.make_async_remote_copy(
                src_ref=sbuf.at[c, to],
                dst_ref=rbuf.at[c, k - 1],
                send_sem=chip_send.at[c],
                recv_sem=chip_recv.at[c],
                device_id={"tensor": 2 * to + core},
                device_id_type=MESH,
            ).start()
            return carry

        lax.fori_loop(1, chips, send, 0)

    def finish(c):
        arrived = rbuf.at[c]
        pltpu.make_async_copy(arrived, arrived, chip_recv.at[c]).wait()
        total = own[c] + jnp.sum(rbuf[c].astype(F32), axis=0)
        out_ref[c] = total

    def down(c, carry):
        project(c)

        @pl.when(c >= 1)
        def _():
            spread(c - 1)

        @pl.when(c >= 4)
        def _():
            finish(c - 4)

        return carry

    lax.fori_loop(0, chunks, down, 0)
    spread(chunks - 1)
    for c in range(max(chunks - 4, 0), chunks):
        finish(c)

    pltpu.make_async_copy(others, others, id_send).wait()

    def drain(c, carry):
        core_copy(c).wait_send()
        arrived = rbuf.at[c]
        pltpu.make_async_copy(arrived, arrived, chip_send.at[c]).wait()
        return carry

    lax.fori_loop(0, chunks, drain, 0)


def shards(
    n, token_ids, return_ids, token_table, return_table, norm_gain, gate_weight, up_weight, down_weight
):
    d, f = gate_weight.shape
    rows = token_ids.shape[0]
    tokens = rows * n
    half = tokens // 2
    chips = n // 2
    chunk = 2 * WIDE
    chunks = d // chunk
    pairs = d // WIDE
    lanes = up_to(tokens, 128)
    slots = min(pairs + chunks, SLOT_BYTES // (2 * up_to(f, 16) * WIDE * 2))
    any_space = pl.BlockSpec(memory_space=pl.ANY)
    folded = pl.pallas_call(
        functools.partial(kernel, n, slots),
        out_shape=jax.ShapeDtypeStruct((chunks, 16, 128), F32),
        in_specs=[any_space] * 8,
        out_specs=pl.BlockSpec(memory_space=pltpu.VMEM),
        scratch_shapes=[
            pltpu.SMEM((rows,), jnp.int32),
            pltpu.SMEM((rows,), jnp.int32),
            pltpu.VMEM(token_table.shape, BF16),
            pltpu.VMEM(return_table.shape, BF16),
            pltpu.VMEM((1, d), F32),
            pltpu.VMEM((n, 2, lanes), jnp.int32),
            pltpu.VMEM((tokens, d), F32),
            pltpu.VMEM((tokens, d), BF16),
            pltpu.VMEM((slots, 2, f, WIDE), BF16),
            pltpu.VMEM((tokens, f), F32),
            pltpu.VMEM((tokens, f), F32),
            pltpu.VMEM((tokens, f), BF16),
            pltpu.VMEM((chunks, 2, half, chunk), F32),
            pltpu.VMEM((chunks, half, chunk), F32),
            pltpu.VMEM((chips, 16, 128), F32),
            pltpu.VMEM((chunks, 16, 128), F32),
            pltpu.VMEM((chunks, chips, 16, 128), BF16),
            pltpu.VMEM((chunks, chips - 1, 16, 128), BF16),
            pltpu.SemaphoreType.DMA((5,)),
            pltpu.SemaphoreType.DMA((slots, 2)),
            pltpu.SemaphoreType.DMA,
            pltpu.SemaphoreType.DMA,
            pltpu.SemaphoreType.DMA((chunks,)),
            pltpu.SemaphoreType.DMA((chunks,)),
            pltpu.SemaphoreType.DMA((chunks,)),
            pltpu.SemaphoreType.DMA((chunks,)),
        ],
        compiler_params=pltpu.CompilerParams(
            collective_id=0, has_side_effects=True, vmem_limit_bytes=61 * 1024 * 1024
        ),
        cost_estimate=pl.CostEstimate(
            flops=6 * tokens * d * f, bytes_accessed=6 * d * f, transcendentals=tokens * f
        ),
    )(
        token_ids,
        return_ids,
        token_table,
        return_table,
        norm_gain.reshape(1, d),
        gate_weight.T,
        up_weight.T,
        down_weight,
    )
    per = 16 // rows
    parts = folded.reshape(chunks, per, rows, 128).transpose(2, 0, 1, 3)
    return parts.reshape(rows, d).astype(BF16)


def solution(mesh):
    in_specs = (
        P(("groups", "tensor")),
        P(("groups", "tensor")),
        P(),
        P(),
        P(),
        P(None, "tensor"),
        P(None, "tensor"),
        P("tensor", None),
    )
    out_specs = P(("groups", "tensor"), None)
    return jax.shard_map(
        functools.partial(shards, mesh.shape["tensor"]),
        mesh=mesh,
        in_specs=in_specs,
        out_specs=out_specs,
        check_vma=False,
    )
```

```python
import functools

import jax
import jax.numpy as jnp
from jax import lax
from jax.experimental import pallas as pl
from jax.experimental.pallas import tpu as pltpu
from jax.sharding import PartitionSpec as P

MESH = pl.DeviceIdType.MESH
F32 = jnp.float32
BF16 = jnp.bfloat16
WIDE = 2048
SLOT_BYTES = 52 * 1024 * 1024


def up_to(value, step):
    return -(-value // step) * step


def kernel(
    n,
    slots,
    tok_hbm,
    ret_hbm,
    tt_hbm,
    rt_hbm,
    gain_hbm,
    gate_hbm,
    up_hbm,
    down_hbm,
    out_ref,
    tok_s,
    ret_s,
    tt,
    rt,
    gain,
    idbuf,
    stream,
    normed,
    weights,
    acc_g,
    acc_u,
    hidden,
    part,
    crecv,
    turned,
    own,
    sbuf,
    rbuf,
    local_sem,
    w_sem,
    id_send,
    id_recv,
    core_send,
    core_recv,
    chip_send,
    chip_recv,
):
    me = lax.axis_index("tensor")
    core = lax.rem(me, 2)
    chip = lax.div(me, 2)
    partner = me + 1 - 2 * core
    chips = n // 2
    rows = tok_hbm.shape[0]
    tokens = rows * n
    half = tokens // 2
    d = gain.shape[1]
    blocks = d // WIDE
    per = 16 // rows
    chunk = per * 128
    chunks = d // chunk
    pieces = WIDE // chunk
    lanes = idbuf.shape[2]

    tok_copy = pltpu.make_async_copy(tok_hbm, tok_s, local_sem.at[0])
    ret_copy = pltpu.make_async_copy(ret_hbm, ret_s, local_sem.at[1])
    tt_copy = pltpu.make_async_copy(tt_hbm, tt, local_sem.at[2])
    rt_copy = pltpu.make_async_copy(rt_hbm, rt, local_sem.at[3])
    gain_copy = pltpu.make_async_copy(gain_hbm, gain, local_sem.at[4])
    tok_copy.start()
    ret_copy.start()

    barrier = pltpu.get_barrier_semaphore()

    def greet(k, carry):
        pl.semaphore_signal(
            barrier, inc=1, device_id={"tensor": lax.rem(me + k, n)}, device_id_type=MESH
        )
        return carry

    lax.fori_loop(1, n, greet, 0)
    tt_copy.start()
    rt_copy.start()
    gain_copy.start()

    def piece(ref, block, slot, which):
        at = pl.ds(pl.multiple_of(block * WIDE + which * chunk, chunk), chunk)
        return pltpu.make_async_copy(
            ref.at[:, at],
            weights.at[slot, :, pl.ds(which * chunk, chunk)],
            w_sem.at[slot, which],
        )

    def start_block(ref, block, t):
        for which in range(pieces):
            piece(ref, block, lax.rem(t, slots), which).start()

    def start_first(t):
        if t < 2 * blocks:
            start_block((gate_hbm, up_hbm)[t % 2], jnp.int32(t // 2), jnp.int32(t))
        else:
            start_block(down_hbm, jnp.int32(t - 2 * blocks), jnp.int32(t))

    start_first(0)

    tok_copy.wait()
    ret_copy.wait()
    lane = lax.broadcasted_iota(jnp.int32, (1, lanes), 1)
    place = core * half + chip * rows
    for kind, ids in ((0, tok_s), (1, ret_s)):
        row = jnp.zeros((1, lanes), jnp.int32)
        for i in range(rows):
            row = jnp.where(lane == place + i, ids[i], row)
        idbuf[n - 1, kind : kind + 1, :] = row

    pl.semaphore_wait(barrier, n - 1)

    def send_ids(k, carry):
        pltpu.make_async_remote_copy(
            src_ref=idbuf.at[n - 1],
            dst_ref=idbuf.at[k - 1],
            send_sem=id_send,
            recv_sem=id_recv,
            device_id={"tensor": lax.rem(me + k, n)},
            device_id_type=MESH,
        ).start()
        return carry

    lax.fori_loop(1, n, send_ids, 0)
    for t in range(1, slots):
        start_first(t)
    tt_copy.wait()
    rt_copy.wait()
    gain_copy.wait()
    others = idbuf.at[pl.ds(0, n - 1)]
    pltpu.make_async_copy(others, others, id_recv).wait()
    both = jnp.sum(idbuf[...], axis=0)

    def one_hot(row, size):
        key = lax.broadcasted_iota(jnp.int32, (128, lanes), 0)
        hot = jnp.where(key == jnp.broadcast_to(row, (128, lanes)), 1.0, 0.0).astype(F32)
        return jnp.transpose(hot)[:tokens, :size].astype(BF16)

    tok_hot = one_hot(both[0:1], tt.shape[0])
    ret_hot = one_hot(both[1:2], rt.shape[0])
    total = jnp.zeros((tokens, 1), F32)
    for c in range(chunks):
        at = slice(c * chunk, (c + 1) * chunk)
        value = jnp.dot(tok_hot, tt[:, at], preferred_element_type=F32) + jnp.dot(
            ret_hot, rt[:, at], preferred_element_type=F32
        )
        stream[:, at] = value
        total += jnp.sum(value * value, axis=1, keepdims=True)
    scale = lax.rsqrt(total / d + 1e-06)
    for c in range(chunks):
        at = slice(c * chunk, (c + 1) * chunk)
        normed[:, at] = (stream[:, at] * scale * gain[:, at]).astype(BF16)

    acc_g[...] = jnp.zeros_like(acc_g)
    acc_u[...] = jnp.zeros_like(acc_u)

    def gate_up(block, carry):
        x = normed[:, pl.ds(pl.multiple_of(block * WIDE, WIDE), WIDE)]
        for kind, ref, acc in ((0, gate_hbm, acc_g), (1, up_hbm, acc_u)):
            t = 2 * block + kind
            slot = lax.rem(t, slots)
            for which in range(pieces):
                piece(ref, block, slot, which).wait()
            acc[...] += lax.dot_general(
                x, weights[slot], (((1,), (1,)), ((), ())), preferred_element_type=F32
            )
            ahead = t + slots

            @pl.when(ahead < 2 * blocks)
            def _():
                start_block((gate_hbm, up_hbm)[(kind + slots) % 2], lax.div(ahead, 2), ahead)

            @pl.when(jnp.logical_and(ahead >= 2 * blocks, ahead < 3 * blocks))
            def _():
                start_block(down_hbm, ahead - 2 * blocks, ahead)

        return carry

    lax.fori_loop(0, blocks, gate_up, 0)
    gate = acc_g[...]
    hidden[...] = (gate / (1.0 + jnp.exp(-gate)) * acc_u[...]).astype(BF16)

    def core_copy(c):
        return pltpu.make_async_remote_copy(
            src_ref=part.at[c, 1 - core],
            dst_ref=crecv.at[c],
            send_sem=core_send.at[c],
            recv_sem=core_recv.at[c],
            device_id={"tensor": partner},
            device_id_type=MESH,
        )

    def project(block, which):
        c = block * pieces + which
        slot = lax.rem(block + 2 * blocks, slots)
        piece(down_hbm, block, slot, which).wait()
        value = jnp.dot(
            hidden[...],
            weights[slot, :, which * chunk : (which + 1) * chunk],
            preferred_element_type=F32,
        )
        part[c, 0] = value[:half]
        part[c, 1] = value[half:]
        core_copy(c).start()

    def spread(c):
        core_copy(c).wait_recv()
        mine = part.at[c, core]
        mine[...] += crecv[c]

        def turn(j):
            for q in range(per):
                turned[j, q * rows : (q + 1) * rows, :] = mine[
                    j * rows : (j + 1) * rows, q * 128 : (q + 1) * 128
                ]

        for j in range(chips):
            turn(j)
        own[c] = turned[chip]
        sbuf[c] = turned[...].astype(BF16)

        def send(k, carry):
            to = lax.rem(chip + k, chips)
            pltpu.make_async_remote_copy(
                src_ref=sbuf.at[c, to],
                dst_ref=rbuf.at[c, k - 1],
                send_sem=chip_send.at[c],
                recv_sem=chip_recv.at[c],
                device_id={"tensor": 2 * to + core},
                device_id_type=MESH,
            ).start()
            return carry

        lax.fori_loop(1, chips, send, 0)

    def finish(c):
        arrived = rbuf.at[c]
        pltpu.make_async_copy(arrived, arrived, chip_recv.at[c]).wait()
        total = own[c] + jnp.sum(rbuf[c].astype(F32), axis=0)
        out_ref[c] = total

    def down(block, carry):
        for which in range(pieces):
            project(block, which)
            c = block * pieces + which

            @pl.when(c >= 1)
            def _():
                spread(c - 1)

            @pl.when(c >= 4)
            def _():
                finish(c - 4)

        return carry

    lax.fori_loop(0, blocks, down, 0)
    spread(chunks - 1)
    for c in range(max(chunks - 4, 0), chunks):
        finish(c)

    pltpu.make_async_copy(others, others, id_send).wait()

    def drain(c, carry):
        core_copy(c).wait_send()
        arrived = rbuf.at[c]
        pltpu.make_async_copy(arrived, arrived, chip_send.at[c]).wait()
        return carry

    lax.fori_loop(0, chunks, drain, 0)


def shards(
    n, token_ids, return_ids, token_table, return_table, norm_gain, gate_weight, up_weight, down_weight
):
    d, f = gate_weight.shape
    rows = token_ids.shape[0]
    tokens = rows * n
    half = tokens // 2
    chips = n // 2
    chunk = 16 // rows * 128
    chunks = d // chunk
    lanes = up_to(tokens, 128)
    slots = min(3 * (d // WIDE), SLOT_BYTES // (up_to(f, 16) * WIDE * 2))
    any_space = pl.BlockSpec(memory_space=pl.ANY)
    folded = pl.pallas_call(
        functools.partial(kernel, n, slots),
        out_shape=jax.ShapeDtypeStruct((chunks, 16, 128), F32),
        in_specs=[any_space] * 8,
        out_specs=pl.BlockSpec(memory_space=pltpu.VMEM),
        scratch_shapes=[
            pltpu.SMEM((rows,), jnp.int32),
            pltpu.SMEM((rows,), jnp.int32),
            pltpu.VMEM(token_table.shape, BF16),
            pltpu.VMEM(return_table.shape, BF16),
            pltpu.VMEM((1, d), F32),
            pltpu.VMEM((n, 2, lanes), jnp.int32),
            pltpu.VMEM((tokens, d), F32),
            pltpu.VMEM((tokens, d), BF16),
            pltpu.VMEM((slots, f, WIDE), BF16),
            pltpu.VMEM((tokens, f), F32),
            pltpu.VMEM((tokens, f), F32),
            pltpu.VMEM((tokens, f), BF16),
            pltpu.VMEM((chunks, 2, half, chunk), F32),
            pltpu.VMEM((chunks, half, chunk), F32),
            pltpu.VMEM((chips, 16, 128), F32),
            pltpu.VMEM((chunks, 16, 128), F32),
            pltpu.VMEM((chunks, chips, 16, 128), BF16),
            pltpu.VMEM((chunks, chips - 1, 16, 128), BF16),
            pltpu.SemaphoreType.DMA((5,)),
            pltpu.SemaphoreType.DMA((slots, WIDE // chunk)),
            pltpu.SemaphoreType.DMA,
            pltpu.SemaphoreType.DMA,
            pltpu.SemaphoreType.DMA((chunks,)),
            pltpu.SemaphoreType.DMA((chunks,)),
            pltpu.SemaphoreType.DMA((chunks,)),
            pltpu.SemaphoreType.DMA((chunks,)),
        ],
        compiler_params=pltpu.CompilerParams(
            collective_id=0, has_side_effects=True, vmem_limit_bytes=61 * 1024 * 1024
        ),
        cost_estimate=pl.CostEstimate(
            flops=6 * tokens * d * f, bytes_accessed=6 * d * f, transcendentals=tokens * f
        ),
    )(
        token_ids,
        return_ids,
        token_table,
        return_table,
        norm_gain.reshape(1, d),
        gate_weight.T,
        up_weight.T,
        down_weight,
    )
    per = 16 // rows
    parts = folded.reshape(chunks, per, rows, 128).transpose(2, 0, 1, 3)
    return parts.reshape(rows, d).astype(BF16)


def solution(mesh):
    in_specs = (
        P(("groups", "tensor")),
        P(("groups", "tensor")),
        P(),
        P(),
        P(),
        P(None, "tensor"),
        P(None, "tensor"),
        P("tensor", None),
    )
    out_specs = P(("groups", "tensor"), None)
    return jax.shard_map(
        functools.partial(shards, mesh.shape["tensor"]),
        mesh=mesh,
        in_specs=in_specs,
        out_specs=out_specs,
        check_vma=False,
    )
```

```python
import functools

import jax
import jax.numpy as jnp
from jax import lax
from jax.experimental import pallas as pl
from jax.experimental.pallas import tpu as pltpu
from jax.sharding import PartitionSpec as P

MESH = pl.DeviceIdType.MESH
F32 = jnp.float32
BF16 = jnp.bfloat16
WIDE = 4096
SLOT_BYTES = 52 * 1024 * 1024


def up_to(value, step):
    return -(-value // step) * step


def kernel(
    n,
    slots,
    tok_hbm,
    ret_hbm,
    tt_hbm,
    rt_hbm,
    gain_hbm,
    gate_hbm,
    up_hbm,
    down_hbm,
    out_ref,
    tok_s,
    ret_s,
    tt,
    rt,
    gain,
    idbuf,
    stream,
    normed,
    weights,
    acc_g,
    acc_u,
    hidden,
    part,
    crecv,
    turned,
    own,
    sbuf,
    rbuf,
    local_sem,
    w_sem,
    id_send,
    id_recv,
    core_send,
    core_recv,
    chip_send,
    chip_recv,
):
    me = lax.axis_index("tensor")
    core = lax.rem(me, 2)
    chip = lax.div(me, 2)
    partner = me + 1 - 2 * core
    chips = n // 2
    rows = tok_hbm.shape[0]
    tokens = rows * n
    half = tokens // 2
    d = gain.shape[1]
    blocks = d // WIDE
    per = 16 // rows
    chunk = per * 128
    chunks = d // chunk
    pieces = WIDE // chunk
    lanes = idbuf.shape[2]

    tok_copy = pltpu.make_async_copy(tok_hbm, tok_s, local_sem.at[0])
    ret_copy = pltpu.make_async_copy(ret_hbm, ret_s, local_sem.at[1])
    tt_copy = pltpu.make_async_copy(tt_hbm, tt, local_sem.at[2])
    rt_copy = pltpu.make_async_copy(rt_hbm, rt, local_sem.at[3])
    gain_copy = pltpu.make_async_copy(gain_hbm, gain, local_sem.at[4])
    tok_copy.start()
    ret_copy.start()

    barrier = pltpu.get_barrier_semaphore()

    def greet(k, carry):
        pl.semaphore_signal(
            barrier, inc=1, device_id={"tensor": lax.rem(me + k, n)}, device_id_type=MESH
        )
        return carry

    lax.fori_loop(1, n, greet, 0)
    tt_copy.start()
    rt_copy.start()
    gain_copy.start()

    def piece(ref, block, slot, which):
        at = pl.ds(pl.multiple_of(block * WIDE + which * chunk, chunk), chunk)
        return pltpu.make_async_copy(
            ref.at[:, at],
            weights.at[slot, :, pl.ds(which * chunk, chunk)],
            w_sem.at[slot, which],
        )

    def start_block(ref, block, t):
        for which in range(pieces):
            piece(ref, block, lax.rem(t, slots), which).start()

    def start_first(t):
        if t < 2 * blocks:
            start_block((gate_hbm, up_hbm)[t % 2], jnp.int32(t // 2), jnp.int32(t))
        else:
            start_block(down_hbm, jnp.int32(t - 2 * blocks), jnp.int32(t))

    start_first(0)

    tok_copy.wait()
    ret_copy.wait()
    lane = lax.broadcasted_iota(jnp.int32, (1, lanes), 1)
    place = core * half + chip * rows
    for kind, ids in ((0, tok_s), (1, ret_s)):
        row = jnp.zeros((1, lanes), jnp.int32)
        for i in range(rows):
            row = jnp.where(lane == place + i, ids[i], row)
        idbuf[n - 1, kind : kind + 1, :] = row

    pl.semaphore_wait(barrier, n - 1)

    def send_ids(k, carry):
        pltpu.make_async_remote_copy(
            src_ref=idbuf.at[n - 1],
            dst_ref=idbuf.at[k - 1],
            send_sem=id_send,
            recv_sem=id_recv,
            device_id={"tensor": lax.rem(me + k, n)},
            device_id_type=MESH,
        ).start()
        return carry

    lax.fori_loop(1, n, send_ids, 0)
    for t in range(1, slots):
        start_first(t)
    tt_copy.wait()
    rt_copy.wait()
    gain_copy.wait()
    others = idbuf.at[pl.ds(0, n - 1)]
    pltpu.make_async_copy(others, others, id_recv).wait()
    both = jnp.sum(idbuf[...], axis=0)

    def one_hot(row, size):
        key = lax.broadcasted_iota(jnp.int32, (128, lanes), 0)
        hot = jnp.where(key == jnp.broadcast_to(row, (128, lanes)), 1.0, 0.0).astype(F32)
        return jnp.transpose(hot)[:tokens, :size].astype(BF16)

    tok_hot = one_hot(both[0:1], tt.shape[0])
    ret_hot = one_hot(both[1:2], rt.shape[0])
    total = jnp.zeros((tokens, 1), F32)
    for c in range(chunks):
        at = slice(c * chunk, (c + 1) * chunk)
        value = jnp.dot(tok_hot, tt[:, at], preferred_element_type=F32) + jnp.dot(
            ret_hot, rt[:, at], preferred_element_type=F32
        )
        stream[:, at] = value
        total += jnp.sum(value * value, axis=1, keepdims=True)
    scale = lax.rsqrt(total / d + 1e-06)
    for c in range(chunks):
        at = slice(c * chunk, (c + 1) * chunk)
        normed[:, at] = (stream[:, at] * scale * gain[:, at]).astype(BF16)

    acc_g[...] = jnp.zeros_like(acc_g)
    acc_u[...] = jnp.zeros_like(acc_u)

    def gate_up(block, carry):
        x = normed[:, pl.ds(pl.multiple_of(block * WIDE, WIDE), WIDE)]
        for kind, ref, acc in ((0, gate_hbm, acc_g), (1, up_hbm, acc_u)):
            t = 2 * block + kind
            slot = lax.rem(t, slots)
            for which in range(pieces):
                piece(ref, block, slot, which).wait()
            acc[...] += lax.dot_general(
                x, weights[slot], (((1,), (1,)), ((), ())), preferred_element_type=F32
            )
            ahead = t + slots

            @pl.when(ahead < 2 * blocks)
            def _():
                start_block((gate_hbm, up_hbm)[(kind + slots) % 2], lax.div(ahead, 2), ahead)

            @pl.when(jnp.logical_and(ahead >= 2 * blocks, ahead < 3 * blocks))
            def _():
                start_block(down_hbm, ahead - 2 * blocks, ahead)

        return carry

    lax.fori_loop(0, blocks, gate_up, 0)
    gate = acc_g[...]
    hidden[...] = (gate / (1.0 + jnp.exp(-gate)) * acc_u[...]).astype(BF16)

    def core_copy(c):
        return pltpu.make_async_remote_copy(
            src_ref=part.at[c, 1 - core],
            dst_ref=crecv.at[c],
            send_sem=core_send.at[c],
            recv_sem=core_recv.at[c],
            device_id={"tensor": partner},
            device_id_type=MESH,
        )

    def project(block, which):
        c = block * pieces + which
        slot = lax.rem(block + 2 * blocks, slots)
        piece(down_hbm, block, slot, which).wait()
        value = jnp.dot(
            hidden[...],
            weights[slot, :, which * chunk : (which + 1) * chunk],
            preferred_element_type=F32,
        )
        part[c, 0] = value[:half]
        part[c, 1] = value[half:]
        core_copy(c).start()

    def spread(c):
        core_copy(c).wait_recv()
        mine = part.at[c, core]
        mine[...] += crecv[c]

        def turn(j):
            for q in range(per):
                turned[j, q * rows : (q + 1) * rows, :] = mine[
                    j * rows : (j + 1) * rows, q * 128 : (q + 1) * 128
                ]

        for j in range(chips):
            turn(j)
        own[c] = turned[chip]
        sbuf[c] = turned[...].astype(BF16)

        def send(k, carry):
            to = lax.rem(chip + k, chips)
            pltpu.make_async_remote_copy(
                src_ref=sbuf.at[c, to],
                dst_ref=rbuf.at[c, k - 1],
                send_sem=chip_send.at[c],
                recv_sem=chip_recv.at[c],
                device_id={"tensor": 2 * to + core},
                device_id_type=MESH,
            ).start()
            return carry

        lax.fori_loop(1, chips, send, 0)

    def finish(c):
        arrived = rbuf.at[c]
        pltpu.make_async_copy(arrived, arrived, chip_recv.at[c]).wait()
        total = own[c] + jnp.sum(rbuf[c].astype(F32), axis=0)
        out_ref[c] = total

    def down(block, carry):
        for which in range(pieces):
            project(block, which)
            c = block * pieces + which

            @pl.when(c >= 1)
            def _():
                spread(c - 1)

            @pl.when(c >= 4)
            def _():
                finish(c - 4)

        return carry

    lax.fori_loop(0, blocks, down, 0)
    spread(chunks - 1)
    for c in range(max(chunks - 4, 0), chunks):
        finish(c)

    pltpu.make_async_copy(others, others, id_send).wait()

    def drain(c, carry):
        core_copy(c).wait_send()
        arrived = rbuf.at[c]
        pltpu.make_async_copy(arrived, arrived, chip_send.at[c]).wait()
        return carry

    lax.fori_loop(0, chunks, drain, 0)


def shards(
    n, token_ids, return_ids, token_table, return_table, norm_gain, gate_weight, up_weight, down_weight
):
    d, f = gate_weight.shape
    rows = token_ids.shape[0]
    tokens = rows * n
    half = tokens // 2
    chips = n // 2
    chunk = 16 // rows * 128
    chunks = d // chunk
    lanes = up_to(tokens, 128)
    slots = min(3 * (d // WIDE), SLOT_BYTES // (up_to(f, 16) * WIDE * 2))
    any_space = pl.BlockSpec(memory_space=pl.ANY)
    folded = pl.pallas_call(
        functools.partial(kernel, n, slots),
        out_shape=jax.ShapeDtypeStruct((chunks, 16, 128), F32),
        in_specs=[any_space] * 8,
        out_specs=pl.BlockSpec(memory_space=pltpu.VMEM),
        scratch_shapes=[
            pltpu.SMEM((rows,), jnp.int32),
            pltpu.SMEM((rows,), jnp.int32),
            pltpu.VMEM(token_table.shape, BF16),
            pltpu.VMEM(return_table.shape, BF16),
            pltpu.VMEM((1, d), F32),
            pltpu.VMEM((n, 2, lanes), jnp.int32),
            pltpu.VMEM((tokens, d), F32),
            pltpu.VMEM((tokens, d), BF16),
            pltpu.VMEM((slots, f, WIDE), BF16),
            pltpu.VMEM((tokens, f), F32),
            pltpu.VMEM((tokens, f), F32),
            pltpu.VMEM((tokens, f), BF16),
            pltpu.VMEM((chunks, 2, half, chunk), F32),
            pltpu.VMEM((chunks, half, chunk), F32),
            pltpu.VMEM((chips, 16, 128), F32),
            pltpu.VMEM((chunks, 16, 128), F32),
            pltpu.VMEM((chunks, chips, 16, 128), BF16),
            pltpu.VMEM((chunks, chips - 1, 16, 128), BF16),
            pltpu.SemaphoreType.DMA((5,)),
            pltpu.SemaphoreType.DMA((slots, WIDE // chunk)),
            pltpu.SemaphoreType.DMA,
            pltpu.SemaphoreType.DMA,
            pltpu.SemaphoreType.DMA((chunks,)),
            pltpu.SemaphoreType.DMA((chunks,)),
            pltpu.SemaphoreType.DMA((chunks,)),
            pltpu.SemaphoreType.DMA((chunks,)),
        ],
        compiler_params=pltpu.CompilerParams(
            collective_id=0, has_side_effects=True, vmem_limit_bytes=61 * 1024 * 1024
        ),
        cost_estimate=pl.CostEstimate(
            flops=6 * tokens * d * f, bytes_accessed=6 * d * f, transcendentals=tokens * f
        ),
    )(
        token_ids,
        return_ids,
        token_table,
        return_table,
        norm_gain.reshape(1, d),
        gate_weight.T,
        up_weight.T,
        down_weight,
    )
    per = 16 // rows
    parts = folded.reshape(chunks, per, rows, 128).transpose(2, 0, 1, 3)
    return parts.reshape(rows, d).astype(BF16)


def solution(mesh):
    in_specs = (
        P(("groups", "tensor")),
        P(("groups", "tensor")),
        P(),
        P(),
        P(),
        P(None, "tensor"),
        P(None, "tensor"),
        P("tensor", None),
    )
    out_specs = P(("groups", "tensor"), None)
    return jax.shard_map(
        functools.partial(shards, mesh.shape["tensor"]),
        mesh=mesh,
        in_specs=in_specs,
        out_specs=out_specs,
        check_vma=False,
    )
```
